32 devices in a mesh: ctx: 2 (over x), exp: 16 (over z, y, core).
Axes of the slice: x: 2, y: 2, z: 4, core: 2. Of those that a mesh axis runs over, the one named last changes fastest.
Arguments:
- tokens: bfloat16 [256, 4096], P('ctx', 'exp'), may hold values from -6 to 6
- input_weight: bfloat16 [4096, 8192], P('ctx', 'exp'), may hold values from -0.09375 to 0.09375
- gate_weight: bfloat16 [4096, 8192], P('ctx', 'exp'), may hold values from -0.09375 to 0.09375
- conv_weight: float32 [4, 8192], P(None, 'exp'), may hold values from -3 to 3
- conv_bias: float32 [8192], P('exp'), may hold values from -3 to 3
- state_weight: bfloat16 [8192, 32], P('exp'), may hold values from -0.0078125 to 0.0078125
- step_size: float32 [256, 8192], P('ctx', 'exp'), may hold values from 0 to 1, as said below
- skip_gain: float32 [8192], P('exp'), may hold values from 0.5 to 2
- output_weight: bfloat16 [8192, 4096], P('exp', 'ctx'), may hold values from -0.0625 to 0.0625
- norm_gain: float32 [4096], replicated, may hold values from 0.1 to 1.9
- router_weight: bfloat16 [4096, 16], replicated, may hold values from -0.09375 to 0.09375
- expert_gate: bfloat16 [16, 7168, 4096], P('exp', 'ctx'), may hold values from -0.09375 to 0.09375
- expert_up: bfloat16 [16, 7168, 4096], P('exp', 'ctx'), may hold values from -0.09375 to 0.09375
- expert_down: bfloat16 [16, 7168, 4096], P('exp', 'ctx'), may hold values from -0.0625 to 0.0625
- expert_ids: int32 [256, 2], P(('ctx', 'exp')), may hold values from 0 to 15, all different within a row; in each aligned block of 8 rows (0 to 7, 8 to 15, ...) at most 2 rows name the same one
Outputs:
- layer_out: bfloat16 [256, 4096], P(('ctx', 'exp'))
The draws below stay inside these ranges and needn't reach their ends.
Inputs may be any that keep to these rules, and one draw needn't show every extreme that they name: `expert_ids`: each token names 2 different experts; in each aligned block of 8 tokens no expert is named by more than 2 tokens. `step_size`: a positive rate for each token and channel.
All inputs are finite; a program needn't handle non-finite values.
Results may differ from the reference program's by a relative error of at most 0.028.
Values may be sent and summed in bfloat16 or wider, within the bound.
No kernel may reach another device: no remote copies, remote signals or barrier semaphores. Data moves between devices by JAX's collectives and lax.ppermute only.
A program may use at most 192 MiB of HBM per device.

```python
import math
import jax
import jax.numpy as jnp
import numpy as np
from jax import lax

D = 4096
INNER_CHANNELS = 8192
STATE = 16
CONV = 4
EF = 7168
TOP = 2
CAP = 2
STRETCH = 128
EXPERTS = 16
TEXT_LEN_ITEMS = 256
ROWS = 8
N_EXP = 16


def draw_step_size(key, part):
    divided_seed_handles = jax.random.split(key, 7)
    slow_share = 0.5
    is_slow = jax.random.bernoulli(divided_seed_handles[0], slow_share, (INNER_CHANNELS,))
    slow_rate = jnp.exp(jax.random.uniform(divided_seed_handles[1], (INNER_CHANNELS,), jnp.float32, math.log(0.08), math.log(0.5))) / TEXT_LEN_ITEMS
    fast_rate = jnp.exp(jax.random.uniform(divided_seed_handles[2], (INNER_CHANNELS,), jnp.float32, math.log(1.0 / 50.0), math.log(1.0 / 30.0)))
    baseline_rate = jnp.where(is_slow, slow_rate, fast_rate)
    jaggedness = jnp.exp(jax.random.uniform(divided_seed_handles[3], (TEXT_LEN_ITEMS, INNER_CHANNELS), jnp.float32, math.log(0.5), math.log(2.0)))
    phase_shift = jax.random.uniform(divided_seed_handles[4], (), jnp.float32, 0.0, 2.0 * math.pi)
    along_sequence = jnp.arange(TEXT_LEN_ITEMS, dtype=jnp.float32) / TEXT_LEN_ITEMS
    position_multiplier = jnp.exp(0.7 * jnp.sin(6.0 * math.pi * along_sequence + phase_shift))
    surge_onset_index = jax.random.randint(divided_seed_handles[5], (2,), 0, TEXT_LEN_ITEMS)
    surge_entries = jnp.any(jnp.arange(TEXT_LEN_ITEMS, dtype=jnp.int32)[:, None] == surge_onset_index[None, :], 1).astype(jnp.float32)
    spike_length = jax.random.uniform(divided_seed_handles[6], (TEXT_LEN_ITEMS, INNER_CHANNELS), jnp.float32, math.log(1.25), math.log(2.0))
    return baseline_rate[None, :] * jaggedness * position_multiplier[:, None] + surge_entries[:, None] * spike_length


def levels(stream_key, shape, shards, smallest, high):
    factor_of, own = 1.0, jax.random.fold_in(stream_key, 6)
    for axis_at, shards_of in shards:
        heights = jnp.exp(jax.random.uniform(jax.random.fold_in(own, axis_at), (shards_of,), jnp.float32, smallest / len(shards), high / len(shards)))
        factor_of = factor_of * jnp.repeat(heights, shape[axis_at] // shards_of).reshape([-1 if axis == axis_at else 1 for axis in range(len(shape))])
    return factor_of


def shared_out(own_key, own, number, rows, number_of, top, bound, lean):
    ranking = jax.random.permutation(own_key, number_of)
    packed, usual = load_shares(number_of, rows * top, bound, lean, True), load_shares(number_of, rows * top, bound, lean, False)
    places = jnp.arange(number_of)

    def named(sizes, turn):
        used = int((sizes > 0).sum())
        fixed = max(1, used // 4)
        moved = fixed + (places - fixed + turn * (used - fixed)) % max(1, number_of - fixed)
        return jnp.zeros((number_of,), jnp.int32).at[ranking[jnp.where(places < fixed, places, moved)]].set(jnp.asarray(sizes, jnp.int32))

    sizes = jnp.where(number % 4 == 0, named(packed, number // 4), named(usual, number - number // 4 - 1))
    mixed = jax.random.permutation(jax.random.fold_in(own, 3), number_of)
    giver, taker = mixed[0:number_of // 2 * 2:2], mixed[1:number_of // 2 * 2:2]
    margin = jnp.minimum(sizes[giver] - 1, bound - sizes[taker]) // 2
    margin = jnp.where((giver == ranking[0]) | (taker == ranking[0]) | (sizes[taker] == 0), 0, jnp.maximum(margin, 0))
    moved = jax.random.randint(jax.random.fold_in(own, 4), (number_of // 2,), 0, 1 << 20) % (margin + 1)
    sizes = sizes.at[giver].add(-moved).at[taker].add(moved)
    labels = jnp.searchsorted(jnp.cumsum(sizes), jnp.arange(rows * top), side="right").astype(jnp.int32)
    listing = labels.reshape(top, rows).T
    listing = listing[jax.random.permutation(jax.random.fold_in(own, 1), rows)]
    turn = jax.random.randint(jax.random.fold_in(own, 2), (rows, 1), 0, top)
    return jnp.take_along_axis(listing, (jnp.arange(top)[None, :] + turn) % top, axis=1)


def load_shares(count, total, most, lean, full):
    loads = [(1 << 20) // math.isqrt(rank ** lean) + 1 for rank in range(1, count + 1)]
    largest = most if full else min(most, max(-(-total // count), total * loads[0] // sum(loads)))
    least = 1 if total - largest >= count - 1 else 0
    counts, rest = [largest] + [least] * (count - 1), total - largest - least * (count - 1)
    while rest > 0:
        candidates = [i for i in range(1, count) if counts[i] < largest] or [i for i in range(1, count) if counts[i] < most]
        pool, budget = sum([loads[i] for i in candidates]), rest
        for i in candidates:
            more = min(most - counts[i], max(1, budget * loads[i] // pool), rest)
            counts[i] = counts[i] + more
            rest = rest - more
    return np.array(counts)


def noise(stream_key, extent, deviation, bound, shards=(), held_as=jnp.bfloat16):
    factor_of = levels(stream_key, extent, shards, -0.22, 0.18) if shards else 1.0
    array = jax.random.normal(stream_key, extent, jnp.float32) * deviation * factor_of
    return jnp.minimum(jnp.maximum(array, -bound), bound).astype(held_as)


def setup_inputs(seed: int = 0) -> dict:
    key_list = jax.random.split(jax.random.key(seed), 16)
    tokens = noise(key_list[0], (TEXT_LEN_ITEMS, D), 1.0, 6.0, ((0, 2), (1, 16)))
    input_weight = noise(key_list[1], (D, INNER_CHANNELS), D ** -0.5, 0.09375, ((0, 2), (1, 16)))
    gate_weight = noise(key_list[2], (D, INNER_CHANNELS), D ** -0.5, 0.09375, ((0, 2), (1, 16)))
    conv_weight = noise(key_list[3], (CONV, INNER_CHANNELS), 0.5, 3.0, ((1, 16),), jnp.float32)
    conv_bias = noise(key_list[4], (INNER_CHANNELS,), 0.5, 3.0, ((0, 16),), jnp.float32)
    state_weight = noise(key_list[5], (INNER_CHANNELS, 2 * STATE), (64 * INNER_CHANNELS) ** -0.5, 0.0078125, ((0, 16),))
    step_size = draw_step_size(jax.random.fold_in(key_list[15], 71), 0)
    skip_gain = jnp.clip(0.5 + 1.5 * jax.random.uniform(key_list[7], (INNER_CHANNELS,), jnp.float32) ** levels(key_list[7], (INNER_CHANNELS,), ((0, 16),), -0.2, 0.2), 0.5, 2.0)
    output_weight = noise(key_list[8], (INNER_CHANNELS, D), INNER_CHANNELS ** -0.5, 0.0625, ((0, 16), (1, 2)))
    norm_gain = jnp.clip(1.0 + 0.18 * jax.random.normal(key_list[9], (D,), jnp.float32), 0.1, 1.9)
    router_weight = noise(key_list[10], (D, EXPERTS), D ** -0.5, 0.09375)
    expert_gate = noise(key_list[11], (EXPERTS, EF, D), D ** -0.5, 0.09375, ((0, 16), (1, 2)))
    expert_up = noise(key_list[12], (EXPERTS, EF, D), D ** -0.5, 0.09375, ((0, 16), (1, 2)))
    expert_down = noise(key_list[13], (EXPERTS, EF, D), EF ** -0.5, 0.0625, ((0, 16), (1, 2)))
    expert_ids_keys = jax.random.split(jax.random.fold_in(key_list[14], 1), TEXT_LEN_ITEMS // (STRETCH // N_EXP))
    expert_ids_turns = jax.random.permutation(jax.random.fold_in(key_list[14], 3), TEXT_LEN_ITEMS // (STRETCH // N_EXP))
    expert_ids = jax.vmap(lambda own, number: shared_out(jax.random.fold_in(key_list[14], 2), own, number, STRETCH // N_EXP, EXPERTS, TOP, CAP, 2))(expert_ids_keys, expert_ids_turns).reshape((TEXT_LEN_ITEMS, TOP))
    return {"tokens": tokens, "input_weight": input_weight, "gate_weight": gate_weight, "conv_weight": conv_weight, "conv_bias": conv_bias, "state_weight": state_weight, "step_size": step_size, "skip_gain": skip_gain, "output_weight": output_weight, "norm_gain": norm_gain, "router_weight": router_weight, "expert_gate": expert_gate, "expert_up": expert_up, "expert_down": expert_down, "expert_ids": expert_ids}


precise = lax.Precision.HIGHEST

def reference(tokens, input_weight, gate_weight, conv_weight, conv_bias, state_weight, step_size, skip_gain, output_weight, norm_gain, router_weight, expert_gate, expert_up, expert_down, expert_ids):
    inner_x = jnp.dot(tokens, input_weight, preferred_element_type=jnp.float32).astype(jnp.bfloat16)
    inner_z = jnp.dot(tokens, gate_weight, preferred_element_type=jnp.float32).astype(jnp.bfloat16)
    extended = jnp.concatenate([jnp.zeros((CONV - 1, INNER_CHANNELS), jnp.bfloat16), inner_x], 0).astype(jnp.float32)
    filtered = jnp.broadcast_to(conv_bias[None, :], (TEXT_LEN_ITEMS, INNER_CHANNELS))
    for offset in range(CONV):
        filtered = filtered + conv_weight[offset][None, :] * extended[offset:offset + TEXT_LEN_ITEMS]
    mixer_in = jax.nn.silu(filtered).astype(jnp.bfloat16)
    mixer_wide = mixer_in.astype(jnp.float32)
    projections = jnp.dot(mixer_in, state_weight, preferred_element_type=jnp.float32)
    input_gain = projections[:, :STATE]
    readout = projections[:, STATE:]
    keep_rate = jnp.exp(-step_size)

    def advance(state, inputs):
        keep_row, incoming_vector, gain_row, read_row = inputs
        state = keep_row[:, None] * state + incoming_vector[:, None] * gain_row[None, :]
        return (state, jnp.dot(state, read_row, precision=precise))
    empty_state = jnp.zeros((INNER_CHANNELS, STATE), jnp.float32)
    readings = lax.scan(advance, empty_state, (keep_rate, mixer_wide, input_gain, readout))[1]
    mixed_state = (readings + skip_gain[None, :] * mixer_wide) * jax.nn.silu(inner_z.astype(jnp.float32))
    blender_result = mixed_state.astype(jnp.bfloat16)
    projected = jnp.dot(blender_result, output_weight, preferred_element_type=jnp.float32)
    residual = (tokens.astype(jnp.float32) + projected).astype(jnp.bfloat16)
    stream = residual.astype(jnp.float32)
    normed = (stream * lax.rsqrt(lax.optimization_barrier(jnp.mean(stream * stream, -1, keepdims=True)) + 1e-05) * norm_gain[None, :]).astype(jnp.bfloat16)
    logits = jnp.dot(normed, router_weight, preferred_element_type=jnp.float32)
    chosen = expert_ids[:, :, None] == jnp.arange(EXPERTS, dtype=jnp.int32)[None, None, :]
    selected_entry = lax.optimization_barrier(jnp.sum(jnp.where(chosen, logits[:, None, :], 0.0), -1))
    shares = jax.nn.sigmoid(selected_entry - selected_entry[:, ::-1])
    slot_bound = CAP * (TEXT_LEN_ITEMS // ROWS)
    positions = jnp.arange(slot_bound, dtype=jnp.int32)

    def one_expert(totals, expert):
        routed = expert_ids == expert
        present = jnp.any(routed, 1)
        weight = lax.optimization_barrier(jnp.sum(jnp.where(routed, shares, 0.0), 1))
        token_index = jnp.nonzero(present, size=slot_bound, fill_value=0)[0].astype(jnp.int32)
        valid_slot = positions < jnp.sum(present.astype(jnp.int32))
        rows_in = normed[token_index].astype(jnp.float32)
        gate_value = jnp.dot(rows_in, expert_gate[expert].astype(jnp.float32).T, precision=precise)
        up_value = jnp.dot(rows_in, expert_up[expert].astype(jnp.float32).T, precision=precise)
        hidden = (jax.nn.silu(gate_value) * up_value).astype(jnp.bfloat16)
        output = jnp.dot(hidden.astype(jnp.float32), expert_down[expert].astype(jnp.float32), precision=precise).astype(jnp.bfloat16)
        weighted = jnp.where(valid_slot[:, None], weight[token_index][:, None] * output.astype(jnp.float32), 0.0)
        return (totals.at[token_index].add(weighted), None)
    moe_out = lax.scan(one_expert, jnp.zeros((TEXT_LEN_ITEMS, D), jnp.float32), jnp.arange(EXPERTS, dtype=jnp.int32))[0]
    return (stream + moe_out).astype(jnp.bfloat16)
```

```python
import jax
import jax.numpy as jnp
from jax import lax
from jax.experimental import pallas as pl
from jax.experimental.pallas import tpu as pltpu
from jax.sharding import PartitionSpec as P

STATE = 16
CONV = 4
TOP = 2
CAP = 2
CHUNK = 64

precise = lax.Precision.HIGHEST
f32 = jnp.float32
bf16 = jnp.bfloat16


def partner(shard, axis, mask):
    devices = lax.axis_size(axis)
    return lax.ppermute(shard, axis, [(i, i ^ mask) for i in range(devices)])


def gather_bit(shard, axis, mask):
    other = partner(shard, axis, mask)
    high = (lax.axis_index(axis) & mask) != 0
    return jnp.stack([jnp.where(high, other, shard), jnp.where(high, shard, other)], 0)


def swap(pieces, axis):
    if lax.axis_size(axis) != 2:
        return lax.all_to_all(pieces, axis, split_axis=0, concat_axis=0, tiled=True)
    me = lax.axis_index(axis)
    own = lax.dynamic_index_in_dim(pieces, me, 0, keepdims=False)
    other = partner(lax.dynamic_index_in_dim(pieces, 1 - me, 0, keepdims=False), axis, 1)
    return jnp.stack([jnp.where(me == 0, own, other), jnp.where(me == 0, other, own)], 0)


def swap_sum(pieces, axis):
    if lax.axis_size(axis) != 2:
        got = lax.all_to_all(pieces.astype(bf16), axis, split_axis=0, concat_axis=0, tiled=True)
        return jnp.sum(got.astype(f32), 0)
    me = lax.axis_index(axis)
    own = lax.dynamic_index_in_dim(pieces, me, 0, keepdims=False)
    leaving = lax.dynamic_index_in_dim(pieces, 1 - me, 0, keepdims=False).astype(bf16)
    return own.astype(f32) + partner(leaving, axis, 1).astype(f32)


def gather_ctx(shard):
    if lax.axis_size("ctx") == 2:
        return gather_bit(shard, "ctx", 1)
    return lax.all_gather(shard, "ctx", axis=0)


def sum_all(value):
    for mask in [1 << b for b in range(lax.axis_size("exp").bit_length() - 1)]:
        value = value + partner(value, "exp", mask)
    for mask in [1 << b for b in range(lax.axis_size("ctx").bit_length() - 1)]:
        value = value + partner(value, "ctx", mask)
    return value


def scan_kernel(mixer_ref, gate_ref, proj_ref, step_ref, skip_ref, out_ref):
    tokens, width = mixer_ref.shape
    chunk = min(CHUNK, tokens)
    rows = lax.broadcasted_iota(jnp.int32, (chunk, chunk), 0)
    columns = lax.broadcasted_iota(jnp.int32, (chunk, chunk), 1)
    causal = rows >= columns
    ones = causal.astype(f32)

    def dot(a, b, dims):
        return lax.dot_general(a, b, (dims, ((), ())), precision=precise, preferred_element_type=f32)

    state = jnp.zeros((STATE, width), f32)
    for start in range(0, tokens, chunk):
        at = pl.ds(start, chunk)
        decay = dot(ones, step_ref[at, :], ((1,), (0,)))
        half = 0.5 * decay[chunk - 1 : chunk, :]
        mixer = mixer_ref[at, :].astype(f32)
        raised = mixer * jnp.exp(decay - half)
        gain = proj_ref[at, :STATE]
        read = proj_ref[at, STATE:]
        scores = jnp.where(causal, dot(read, gain, ((1,), (1,))), 0.0)
        fall = jnp.exp(-half)
        state = state * fall
        reading = jnp.exp(half - decay) * (
            dot(scores, raised, ((1,), (0,))) + dot(read, state, ((1,), (0,)))
        )
        state = fall * (state + dot(gain, raised, ((0,), (0,))))
        gate = gate_ref[at, :].astype(f32)
        mixed = (reading + skip_ref[...] * mixer) * (gate * jax.nn.sigmoid(gate))
        out_ref[at, :] = mixed.astype(out_ref.dtype)


def local(
    tokens,
    input_weight,
    gate_weight,
    conv_weight,
    conv_bias,
    state_weight,
    step_size,
    skip_gain,
    output_weight,
    norm_gain,
    router_weight,
    expert_gate,
    expert_up,
    expert_down,
    expert_ids,
):
    nx, ne = lax.axis_size("ctx"), lax.axis_size("exp")
    ctx, exp = lax.axis_index("ctx"), lax.axis_index("exp")
    stretch, part = tokens.shape
    total = stretch * nx
    rows = expert_ids.shape[0]
    width = input_weight.shape[1] // nx

    masks = [1 << b for b in range(ne.bit_length() - 1)]
    outer_bits = max(2, nx.bit_length() - 1)
    inner_masks, outer_masks = masks[: len(masks) - outer_bits], masks[len(masks) - outer_bits :]
    block = tokens
    for mask in outer_masks:
        block = gather_bit(block, "exp", mask)
    outer = 1 << outer_bits
    block = block.reshape(nx, outer // nx, stretch, part)
    block = swap(block, "ctx")
    for mask in reversed(inner_masks):
        block = gather_bit(block, "exp", mask)
    inner = 1 << len(inner_masks)
    lead = len(inner_masks)
    block = block.reshape((2,) * lead + (nx, outer // nx, stretch, part))
    order = (lead, lead + 2, lead + 1) + tuple(reversed(range(lead))) + (lead + 3,)
    everything = block.transpose(order).reshape(total, outer // nx * inner * part)

    inner_x = jnp.dot(everything, input_weight, preferred_element_type=f32)
    inner_x = inner_x.reshape(total, nx, width).transpose(1, 0, 2)
    inner_x = swap_sum(inner_x, "ctx").astype(bf16)
    inner_z = jnp.dot(everything, gate_weight, preferred_element_type=f32)
    inner_z = inner_z.reshape(total, nx, width).transpose(1, 0, 2)
    inner_z = swap_sum(inner_z, "ctx").astype(bf16)

    def mine(array, axis):
        return lax.dynamic_slice_in_dim(array, ctx * width, width, axis)

    extended = jnp.pad(inner_x, ((CONV - 1, 0), (0, 0))).astype(f32)
    taps = mine(conv_weight, 1)
    filtered = jnp.broadcast_to(mine(conv_bias, 0)[None, :], (total, width))
    for offset in range(CONV):
        filtered = filtered + taps[offset][None, :] * extended[offset : offset + total]
    mixer_in = jax.nn.silu(filtered).astype(bf16)
    projections = sum_all(
        jnp.dot(mixer_in, mine(state_weight, 0), preferred_element_type=f32)
    )
    steps = swap(step_size.reshape(stretch, nx, width).transpose(1, 0, 2), "ctx")
    steps = steps.reshape(total, width)
    mixer_out = pl.pallas_call(
        scan_kernel,
        out_shape=jax.ShapeDtypeStruct((total, width), bf16),
        in_specs=[pl.BlockSpec(memory_space=pltpu.VMEM)] * 5,
        out_specs=pl.BlockSpec(memory_space=pltpu.VMEM),
        compiler_params=pltpu.CompilerParams(vmem_limit_bytes=32 * 1024 * 1024),
        name="state_scan",
    )(mixer_in, inner_z, projections, steps, mine(skip_gain, 0)[None, :])

    mixer_out = gather_ctx(mixer_out).transpose(1, 0, 2).reshape(total, nx * width)
    partial = jnp.dot(mixer_out, output_weight, preferred_element_type=f32).astype(bf16)
    columns = partial.shape[1]
    partial = partial.reshape(nx, ne // 2, 2, rows, columns).transpose(2, 1, 0, 3, 4)
    low = exp & 1
    own = lax.dynamic_index_in_dim(partial, low, 0, keepdims=False).astype(f32)
    other = partner(lax.dynamic_index_in_dim(partial, 1 - low, 0, keepdims=False), "exp", 1)
    pair = (own + other.astype(f32)).astype(bf16)
    groups = [[2 * i + k for i in range(ne // 2)] for k in range(2)]
    pieces = lax.all_to_all(
        pair, "exp", split_axis=0, concat_axis=0, tiled=True, axis_index_groups=groups
    )
    projected = jnp.sum(pieces.astype(f32), 0)
    own_tokens = lax.dynamic_index_in_dim(
        everything.reshape(nx, ne, rows, columns), exp, 1, keepdims=False
    )
    residual = (own_tokens.astype(f32) + projected).astype(bf16)

    experts = router_weight.shape[1]
    everyone = gather_ctx(expert_ids)
    chosen = (everyone[..., None] == jnp.arange(experts, dtype=jnp.int32)).astype(jnp.int32)
    hits = chosen.reshape(nx, rows * TOP, experts)
    earlier = jnp.cumsum(hits, 1) - hits
    slot = jnp.sum(earlier * hits, -1).reshape(nx, rows, TOP)
    place = everyone * CAP + slot
    placed = place[..., None] == jnp.arange(experts * CAP, dtype=jnp.int32)
    selector = jnp.any(placed, 2).astype(bf16)
    outgoing = lax.dot_general(
        selector, residual, (((1,), (1,)), ((0,), (0,))), preferred_element_type=f32
    ).astype(bf16)
    outgoing = outgoing.reshape(nx, experts, CAP, columns).transpose(1, 0, 2, 3)
    outgoing = jnp.broadcast_to(outgoing[None], (nx,) + outgoing.shape)
    outgoing = outgoing.reshape(nx * experts, nx * CAP, columns)
    arrived = lax.all_to_all(outgoing, ("ctx", "exp"), split_axis=0, concat_axis=0, tiled=True)
    slots = experts * nx * CAP
    arrived = arrived.reshape(nx, slots, columns).transpose(1, 0, 2).reshape(slots, nx * columns)

    def norm(values):
        wide = values.astype(f32)
        scale = lax.rsqrt(jnp.mean(wide * wide, -1, keepdims=True) + 1e-05)
        return (wide * scale * norm_gain[None, :]).astype(bf16)

    normed = norm(arrived)
    gate_value = lax.dot_general(
        normed, expert_gate[0], (((1,), (1,)), ((), ())), preferred_element_type=f32
    )
    up_value = lax.dot_general(
        normed, expert_up[0], (((1,), (1,)), ((), ())), preferred_element_type=f32
    )
    hidden = (jax.nn.silu(gate_value) * up_value).astype(bf16)
    finished = jnp.dot(hidden, expert_down[0], preferred_element_type=f32).astype(bf16)
    finished = finished.reshape(experts, nx, CAP, -1).transpose(1, 0, 2, 3)
    finished = finished.reshape(nx * experts, CAP, -1)
    returned = lax.all_to_all(finished, ("ctx", "exp"), split_axis=0, concat_axis=0, tiled=True)
    returned = returned.reshape(nx, experts * CAP, -1)
    returned = jnp.sum(returned.astype(f32), 0)

    home = swap(residual, "ctx").transpose(1, 0, 2).reshape(rows, nx * columns)
    logits = jnp.dot(norm(home), router_weight, preferred_element_type=f32)
    my_choice = expert_ids[:, :, None] == jnp.arange(experts, dtype=jnp.int32)
    picked = jnp.sum(jnp.where(my_choice, logits[:, None, :], 0.0), -1)
    shares = jax.nn.sigmoid(picked - picked[:, ::-1])
    my_placed = lax.dynamic_index_in_dim(placed, ctx, 0, keepdims=False)
    combine = jnp.sum(jnp.where(my_placed, shares[:, :, None], 0.0), 1)
    moe_out = jnp.dot(combine, returned, precision=precise)
    return (home.astype(f32) + moe_out).astype(bf16)


def solution(mesh):
    in_specs = (
        P("ctx", "exp"),
        P("ctx", "exp"),
        P("ctx", "exp"),
        P(None, "exp"),
        P("exp"),
        P("exp", None),
        P("ctx", "exp"),
        P("exp"),
        P("exp", "ctx"),
        P(),
        P(),
        P("exp", "ctx", None),
        P("exp", "ctx", None),
        P("exp", "ctx", None),
        P(("ctx", "exp"), None),
    )
    out_specs = P(("ctx", "exp"), None)
    return jax.shard_map(local, mesh=mesh, in_specs=in_specs, out_specs=out_specs, check_vma=False)
```

```python
import functools

import jax
import jax.numpy as jnp
from jax import lax
from jax.experimental import pallas as pl
from jax.experimental.pallas import tpu as pltpu
from jax.sharding import PartitionSpec as P

STATE = 16
CONV = 4
EPS = 1e-05
TOP = 2
CAP = 2
CHUNK = 64
QUARTERS = 8

precise = lax.Precision.HIGHEST
f32 = jnp.float32
bf16 = jnp.bfloat16


VMEM = pl.BlockSpec(memory_space=pltpu.VMEM)
SMEM = pl.BlockSpec(memory_space=pltpu.SMEM)
ANY = pl.BlockSpec(memory_space=pltpu.HBM)
MIB = 1024 * 1024


def limit(total):
    return pltpu.CompilerParams(vmem_limit_bytes=min(48, 8 * max(1, total // 256)) * MIB)


def dot(a, b, dims=((1,), (0,)), precision=None):
    return lax.dot_general(a, b, (dims, ((), ())), precision=precision, preferred_element_type=f32)


def partner(shard, axis, mask):
    devices = lax.axis_size(axis)
    return lax.ppermute(shard, axis, [(i, i ^ mask) for i in range(devices)])


def is_first(where, rank):
    return lax.slice(where, (0,), (1,)).reshape((1,) * rank) == 0


def gather_ctx(shard, where):
    if lax.axis_size("ctx") != 2:
        return lax.all_gather(shard, "ctx", axis=0)
    other = partner(shard, "ctx", 1)
    first = is_first(where, shard.ndim)
    return jnp.stack([jnp.where(first, shard, other), jnp.where(first, other, shard)], 0)


def swap_rows(pieces, where):
    if lax.axis_size("ctx") != 2:
        return lax.all_to_all(pieces, "ctx", split_axis=0, concat_axis=0, tiled=True)
    first = is_first(where, pieces.ndim - 1)
    own = jnp.where(first, pieces[0], pieces[1])
    other = partner(jnp.where(first, pieces[1], pieces[0]), "ctx", 1)
    return jnp.stack([jnp.where(first, own, other), jnp.where(first, other, own)], 0)


def token_planes(tokens):
    return [tokens] + [partner(tokens, "exp", mask) for mask in (4, 8, 12)]


def token_pieces(planes, where):
    size = lax.axis_size("exp")
    ctx, exp = [lax.slice(where, (i,), (i + 1,)).reshape(1, 1) for i in (0, 1)]
    near = ((exp >> 3) & 1) == ctx
    keep = jnp.stack([jnp.where(near, planes[i], planes[i + 2]) for i in (0, 1)], 0)
    give = jnp.stack([jnp.where(near, planes[i + 2], planes[i]) for i in (0, 1)], 0)
    both = [(i, i ^ (size | 2)) for i in range(2 * size)]
    found = {
        (0, 0): keep,
        (1, 0): partner(give, "ctx", 1),
        (0, 1): partner(keep, "exp", 2),
        (1, 1): lax.ppermute(give, ("ctx", "exp"), both),
    }
    pieces = []
    for (dx, dy), piece in found.items():
        pieces.append(((dx, dy, 0), piece))
        pieces.append(((dx, dy, 1), partner(piece, "exp", 1)))
    return pieces


def input_kernel(places, rows, where_ref, *refs):
    pieces, (x_ref, z_ref, x_keep, x_send, z_keep, z_send, own_ref, whole) = refs[:8], refs[8:16]
    weights, arrived = refs[16:]
    copies = [
        pltpu.make_async_copy(ref, weights.at[i], arrived.at[i]) for i, ref in enumerate((x_ref, z_ref))
    ]
    for copy in copies:
        copy.start()
    ctx, exp = where_ref[0], where_ref[1]
    for (dx, dy, dk), piece in zip(places, pieces):
        for j in range(2):
            block = (((exp >> 2) & 1) ^ j) * 4 + (((exp >> 1) & 1) ^ dy) * 2 + ((exp & 1) ^ dk)
            whole[block, ctx ^ dx] = piece[j]
    blocks, _, stretch, part = whole.shape
    everything = jnp.concatenate(
        [whole[b].reshape(2 * stretch, part) for b in range(blocks)], axis=1
    )
    for i, (keep_ref, send_ref) in enumerate(((x_keep, x_send), (z_keep, z_send))):
        copies[i].wait()
        result = dot(everything, weights[i])
        keep_ref[...] = result
        send_ref[...] = result.astype(bf16)
    own_rows = 2 * rows
    row = lax.broadcasted_iota(jnp.int32, (own_rows, 2 * stretch), 0)
    column = lax.broadcasted_iota(jnp.int32, (own_rows, 2 * stretch), 1)
    wanted = jnp.where(row >= rows, row - rows + stretch, row) + exp * rows
    pick = (column == wanted).astype(f32).astype(bf16)
    own_ref[...] = dot(pick, everything).astype(bf16)


def input_call(where, pieces, x_weight, z_weight, rows):
    stretch, part = pieces[0][1].shape[1:]
    shape = (2 * stretch, x_weight.shape[1])
    out_shape = [jax.ShapeDtypeStruct(shape, f32), jax.ShapeDtypeStruct(shape, bf16)] * 2
    out_shape.append(jax.ShapeDtypeStruct((2 * rows, x_weight.shape[0]), bf16))
    places = tuple(place for place, _ in pieces)
    return pl.pallas_call(
        functools.partial(input_kernel, places, rows),
        out_shape=out_shape,
        in_specs=[SMEM] + [VMEM] * 8 + [ANY] * 2,
        out_specs=[VMEM] * len(out_shape),
        scratch_shapes=[
            pltpu.VMEM((8, 2, stretch, part), bf16),
            pltpu.VMEM((2,) + x_weight.shape, bf16),
            pltpu.SemaphoreType.DMA((2,)),
        ],
        compiler_params=pltpu.CompilerParams(vmem_limit_bytes=14 * MIB),
        name="input_projections",
    )(where, *[piece for _, piece in pieces], x_weight, z_weight)


def conv_kernel(
    own_ref, got_ref, taps_ref, bias_ref, project_ref, mixer_ref, part_ref, padded, mixer_held, left
):
    total, width = own_ref.shape
    inner = (own_ref[...] + got_ref[...].astype(f32)).astype(bf16).astype(f32)
    padded[0:8, :] = jnp.zeros((8, width), f32)
    padded[8 : 8 + total, :] = inner
    filtered = jnp.broadcast_to(bias_ref[...], (total, width))
    for offset in range(CONV):
        first = 8 - (CONV - 1) + offset
        filtered = filtered + taps_ref[offset : offset + 1, :] * padded[first : first + total, :]
    mixer = (filtered * jax.nn.sigmoid(filtered)).astype(bf16)
    mixer_held[...] = mixer
    leaving = pltpu.make_async_copy(mixer_held, mixer_ref, left)
    leaving.start()
    part_ref[...] = dot(project_ref[...], mixer, ((1,), (1,)))
    leaving.wait()


def mixer_kernel(
    homes, group, where_ref, proj_ref, skip_ref, mixer_any, step_any, gate_any, got_any, weight_any,
    keep_any, send_ref, columns, mixed, mixer_ref, step_ref, gate_ref, got_ref, weight_ref, keep_ref,
    arrived,
):
    sources = (mixer_any, step_any, gate_any, got_any, weight_any)
    copies = [
        pltpu.make_async_copy(source, ref, arrived.at[i])
        for i, (source, ref) in enumerate(
            zip(sources, (mixer_ref, step_ref, gate_ref, got_ref, weight_ref))
        )
    ]
    for copy in copies:
        copy.start()
    total, width = mixer_ref.shape
    chunk = min(CHUNK, total)
    contexts = total // (homes * group)
    rows = lax.broadcasted_iota(jnp.int32, (chunk, chunk), 0)
    cols = lax.broadcasted_iota(jnp.int32, (chunk, chunk), 1)
    causal = rows >= cols
    ones = causal.astype(f32)
    columns[...] = jnp.sum(proj_ref[...], 0).T
    low = where_ref[1] & 1
    for copy in copies[:4]:
        copy.wait()

    def step(turn, state):
        start = turn * chunk
        at = pl.ds(start if isinstance(start, int) else pl.multiple_of(start, chunk), chunk)
        decay = dot(ones, step_ref[at, :], precision=precise)
        half = 0.5 * decay[chunk - 1 : chunk, :]
        mixer = mixer_ref[at, :].astype(f32)
        raised = mixer * jnp.exp(decay - half)
        gain = columns[at, :STATE]
        read = columns[at, STATE:]
        scores = jnp.where(causal, dot(read, gain, ((1,), (1,)), precise), 0.0)
        fall = jnp.exp(-half)
        state = state * fall
        reading = jnp.exp(half - decay) * (
            dot(scores, raised, precision=precise) + dot(read, state, precision=precise)
        )
        state = fall * (state + dot(gain, raised, ((0,), (0,)), precise))
        gate = (gate_ref[at, :] + got_ref[at, :].astype(f32)).astype(bf16).astype(f32)
        result = (reading + skip_ref[...] * mixer) * (gate * jax.nn.sigmoid(gate))
        for i in range(chunk // group):
            number = turn * (chunk // group) + i
            home, context = number % homes, number // homes
            place = ((home % 2) * (homes // 2) + home // 2) * contexts + context
            place = place * group
            if not isinstance(place, int):
                place = pl.multiple_of(place, group)
            mixed[pl.ds(place, group), :] = result[i * group : (i + 1) * group, :]
        return state

    state = jnp.zeros((STATE, width), f32)
    turns = total // chunk
    if turns <= 4:
        for turn in range(turns):
            state = step(turn, state)
    else:
        lax.fori_loop(0, turns, step, state)
    part = total // 2
    mine = mixed[pl.ds(pl.multiple_of(low * part, part), part), :].astype(bf16)
    other = mixed[pl.ds(pl.multiple_of((1 - low) * part, part), part), :].astype(bf16)
    copies[4].wait()
    keep_ref[...] = dot(mine, weight_ref[...]).astype(bf16)
    leaving = pltpu.make_async_copy(keep_ref, keep_any, arrived.at[5])
    leaving.start()
    send_ref[...] = dot(other, weight_ref[...]).astype(bf16)
    leaving.wait()


def pair_kernel(keep_any, got_ref, out_ref, keep_ref, arrived):
    copy = pltpu.make_async_copy(keep_any, keep_ref, arrived)
    copy.start()
    copy.wait()
    out_ref[...] = (keep_ref[...].astype(f32) + got_ref[...].astype(f32)).astype(bf16)


def dispatch_kernel(parts, pieces_ref, tokens_ref, select_ref, residual_ref, out_ref):
    projected = jnp.sum(pieces_ref[...].astype(f32), 0)
    residual = (tokens_ref[...].astype(f32) + projected).astype(bf16)
    residual_ref[...] = residual
    width = residual.shape[1] // parts
    stacked = jnp.concatenate([residual[:, q * width : (q + 1) * width] for q in range(parts)], 0)
    sent = dot(select_ref[...], stacked).astype(bf16)
    for c in range(out_ref.shape[0]):
        out_ref[c] = sent


def expert_kernel(
    contexts, parts, packed, got_ref, scale_ref, gate_any, up_any, down_any, out_ref,
    inputs, sums, held, arrived,
):
    slots, features = inputs.shape
    depth, _, block, _ = held.shape
    count = gate_any.shape[1] // block

    def copies(step):
        slot = step % depth
        return [
            pltpu.make_async_copy(
                ref.at[0, pl.ds(step * block, block)], held.at[slot, i], arrived.at[slot, i]
            )
            for i, ref in enumerate((gate_any, up_any, down_any))
        ]

    for step in range(min(depth - 1, count)):
        for copy in copies(step):
            copy.start()
    lanes = got_ref.shape[2]
    height = got_ref.shape[1]
    homes = slots // (contexts * CAP)
    row = lax.broadcasted_iota(jnp.int32, (slots, height), 0)
    column = lax.broadcasted_iota(jnp.int32, (slots, height), 1)
    cap, home = row % CAP, (row // CAP) % homes
    context = row // (CAP * homes)
    base = (home * parts * contexts + context) * CAP + cap
    for q in range(parts):
        pick = (column == base + q * contexts * CAP).astype(f32).astype(bf16)
        for c in range(contexts):
            first = (c * parts + q) * lanes
            inputs[:, first : first + lanes] = dot(pick, got_ref[c]).astype(bf16)
    wide = inputs[...].astype(f32)
    scale = lax.rsqrt(jnp.mean(wide * wide, -1, keepdims=True) + EPS)
    inputs[...] = (wide * scale * scale_ref[...]).astype(bf16)
    sums[...] = jnp.zeros_like(sums)

    for step in range(count):
        if step + depth - 1 < count:
            for copy in copies(step + depth - 1):
                copy.start()
        slot = step % depth
        gate_copy, up_copy, down_copy = copies(step)
        tokens = inputs[...]
        gate_copy.wait()
        gate = dot(tokens, held[slot, 0], ((1,), (1,)))
        up_copy.wait()
        up = dot(tokens, held[slot, 1], ((1,), (1,)))
        hidden = (gate * jax.nn.sigmoid(gate) * up).astype(bf16)
        down_copy.wait()
        sums[...] += dot(hidden, held[slot, 2])
    if not packed:
        out_ref[...] = sums[...].astype(bf16)
        return
    finished = sums[...].astype(bf16)
    width = features // QUARTERS
    stacked = jnp.concatenate(
        [finished[:, q * width : (q + 1) * width] for q in range(QUARTERS)], 0
    )
    size = slots * QUARTERS
    row = lax.broadcasted_iota(jnp.int32, (size, size), 0)
    column = lax.broadcasted_iota(jnp.int32, (size, size), 1)
    peer, q, cap = row // (QUARTERS * CAP), (row // CAP) % QUARTERS, row % CAP
    pick = (column == q * slots + peer * CAP + cap).astype(f32).astype(bf16)
    out_ref[...] = dot(pick, stacked).astype(bf16)


def home_kernel(returned_ref, combine_ref, home_ref, out_ref):
    rows = home_ref.shape[0]
    mixed = dot(combine_ref[...], returned_ref[...].astype(f32), precision=precise)
    mixed = jnp.concatenate([mixed[q * rows : (q + 1) * rows, :] for q in range(QUARTERS)], 1)
    out_ref[...] = (home_ref[...].astype(f32) + mixed).astype(bf16)


def local(
    tokens,
    input_weight,
    gate_weight,
    conv_weight,
    conv_bias,
    state_weight,
    step_size,
    skip_gain,
    output_weight,
    norm_gain,
    router_weight,
    expert_gate,
    expert_up,
    expert_down,
    expert_ids,
):
    nx, ne = lax.axis_size("ctx"), lax.axis_size("exp")
    ctx, exp = lax.axis_index("ctx"), lax.axis_index("exp")
    stretch, part = tokens.shape
    total = stretch * nx
    rows = expert_ids.shape[0]
    width = input_weight.shape[1]
    columns = output_weight.shape[1]
    experts = router_weight.shape[1]
    where = lax.optimization_barrier(jnp.stack([ctx, exp]).astype(jnp.int32))

    if nx == 2 and ne == 16:
        planes = token_planes(tokens)
        pieces = token_pieces(planes, where)
        x_own, x_send, z_own, z_send, own_tokens = input_call(
            where, pieces, input_weight, gate_weight, rows
        )
        x_send, step_size, expert_ids = lax.optimization_barrier((x_send, step_size, expert_ids))
        x_got = partner(x_send, "ctx", 1)
        z_got = partner(z_send, "ctx", 1)
    else:
        stretch_whole = lax.all_gather(tokens, "exp", axis=1, tiled=True)
        everything = lax.all_to_all(
            stretch_whole, "ctx", split_axis=1, concat_axis=0, tiled=True
        )
        own_tokens = lax.dynamic_index_in_dim(
            everything.reshape(nx, ne, rows, columns), exp, 1, keepdims=False
        ).reshape(nx * rows, columns)
        x_own = lax.psum(dot(everything, input_weight), "ctx")
        z_own = lax.psum(dot(everything, gate_weight), "ctx")
        x_got = z_got = jnp.zeros((total, width), bf16)

    everyone = gather_ctx(expert_ids, where)
    chosen = (everyone[..., None] == jnp.arange(experts, dtype=jnp.int32)).astype(jnp.int32)
    hits = chosen.reshape(nx, rows * TOP, experts)
    earlier = jnp.cumsum(hits, 1) - hits
    slot = jnp.sum(earlier * hits, -1).reshape(nx, rows, TOP)
    place = everyone * CAP + slot
    placed = place[..., None] == jnp.arange(experts * CAP, dtype=jnp.int32)
    parts = max(1, 16 // (nx * CAP))
    taken = jnp.any(placed, 2).reshape(nx, rows, experts, CAP)
    same_part = jnp.eye(parts, dtype=bool)[None, :, None, None, :, None, None]
    same_ctx = jnp.eye(nx, dtype=bool)[None, None, :, None, None, :, None]
    by_expert = taken.transpose(2, 3, 0, 1)[:, None, None, :, None, :, :]
    select = (by_expert & same_part & same_ctx).astype(bf16)
    slots = experts * nx * CAP
    select = select.reshape(slots * parts, parts * nx * rows)
    steps = gather_ctx(step_size, where).reshape(total, width)

    mixer_in, part_sum = pl.pallas_call(
        conv_kernel,
        out_shape=[
            jax.ShapeDtypeStruct((total, width), bf16),
            jax.ShapeDtypeStruct((2 * STATE, total), f32),
        ],
        in_specs=[VMEM] * 5,
        out_specs=[ANY, VMEM],
        scratch_shapes=[
            pltpu.VMEM((8 + total, width), f32),
            pltpu.VMEM((total, width), bf16),
            pltpu.SemaphoreType.DMA,
        ],
        compiler_params=limit(total),
        name="convolution",
    )(x_own, x_got, conv_weight, conv_bias[None, :], state_weight.T)

    groups = [[2 * i + k for i in range(ne // 2)] for k in range(2)]
    part_sum = part_sum + partner(part_sum, "exp", 1)
    projections = lax.all_to_all(
        jnp.broadcast_to(part_sum[None], (ne // 2,) + part_sum.shape),
        "exp", split_axis=0, concat_axis=0, tiled=True, axis_index_groups=groups,
    )
    projections, select = lax.optimization_barrier((projections, select))
    keep, send = pl.pallas_call(
        functools.partial(mixer_kernel, ne, rows),
        out_shape=[jax.ShapeDtypeStruct((total // 2, columns), bf16)] * 2,
        in_specs=[SMEM] + [VMEM] * 2 + [ANY] * 5,
        out_specs=[ANY, VMEM],
        scratch_shapes=[
            pltpu.VMEM((total, 2 * STATE), f32),
            pltpu.VMEM((total, width), f32),
            pltpu.VMEM((total, width), bf16),
            pltpu.VMEM((total, width), f32),
            pltpu.VMEM((total, width), f32),
            pltpu.VMEM((total, width), bf16),
            pltpu.VMEM(output_weight.shape, bf16),
            pltpu.VMEM((total // 2, columns), bf16),
            pltpu.SemaphoreType.DMA((6,)),
        ],
        compiler_params=limit(2 * total),
        name="state_scan_and_output",
    )(
        where, projections, skip_gain[None, :],
        mixer_in, steps, z_own, z_got, output_weight,
    )

    pair = pl.pallas_call(
        pair_kernel,
        out_shape=jax.ShapeDtypeStruct(send.shape, bf16),
        in_specs=[ANY, VMEM],
        out_specs=VMEM,
        scratch_shapes=[pltpu.VMEM(send.shape, bf16), pltpu.SemaphoreType.DMA],
        compiler_params=limit(total),
        name="pair_sum",
    )(keep, partner(send, "exp", 1))
    sums = lax.all_to_all(
        pair.reshape(ne // 2, nx * rows, columns),
        "exp", split_axis=0, concat_axis=0, tiled=True, axis_index_groups=groups,
    )

    residual, outgoing = pl.pallas_call(
        functools.partial(dispatch_kernel, parts),
        out_shape=[
            jax.ShapeDtypeStruct((nx * rows, columns), bf16),
            jax.ShapeDtypeStruct((nx, slots * parts, columns // parts), bf16),
        ],
        in_specs=[VMEM] * 3,
        out_specs=[VMEM] * 2,
        compiler_params=limit(total),
        name="residual_and_dispatch",
    )(sums, own_tokens, select)
    arrived = lax.all_to_all(
        outgoing.reshape(nx * experts, nx * CAP * parts, columns // parts),
        ("ctx", "exp"), split_axis=0, concat_axis=0, tiled=True,
    ).reshape(nx, slots * parts, columns // parts)

    hidden, features = expert_gate.shape[1:]
    block = next(b for b in (512, 448, 256, 128, 64, 32, 16) if hidden % b == 0)
    packed = nx == 2
    unit = features // QUARTERS
    peers = nx * experts
    done_shape = (peers * CAP * QUARTERS, unit) if packed else (slots, features)
    depth = 3 if packed else 2
    finished = pl.pallas_call(
        functools.partial(expert_kernel, nx, parts, packed),
        out_shape=jax.ShapeDtypeStruct(done_shape, bf16),
        in_specs=[VMEM] * 2 + [ANY] * 3,
        out_specs=VMEM,
        scratch_shapes=[
            pltpu.VMEM((slots, features), bf16),
            pltpu.VMEM((slots, features), f32),
            pltpu.VMEM((depth, 3, block, features), bf16),
            pltpu.SemaphoreType.DMA((depth, 3)),
        ],
        compiler_params=pltpu.CompilerParams(vmem_limit_bytes=52 * MIB),
        cost_estimate=pl.CostEstimate(
            flops=6 * slots * hidden * features,
            bytes_accessed=6 * hidden * features,
            transcendentals=slots * hidden,
        ),
        name="experts",
    )(arrived, norm_gain[None, :], expert_gate, expert_up, expert_down)
    if not packed:
        finished = finished.reshape(peers, CAP, QUARTERS, unit).transpose(0, 2, 1, 3)
    returned = lax.all_to_all(
        finished.reshape(peers, QUARTERS * CAP, unit),
        ("ctx", "exp"), split_axis=0, concat_axis=0, tiled=True,
    ).reshape(peers * QUARTERS * CAP, unit)

    home = swap_rows(residual.reshape(nx, rows, columns), where)
    home = home.transpose(1, 0, 2).reshape(rows, features)
    wide = home.astype(f32)
    scale = lax.rsqrt(jnp.mean(wide * wide, -1, keepdims=True) + EPS)
    normed = (wide * scale * norm_gain[None, :]).astype(bf16)
    logits = dot(normed, router_weight)
    my_choice = expert_ids[:, :, None] == jnp.arange(experts, dtype=jnp.int32)
    picked = jnp.sum(jnp.where(my_choice, logits[:, None, :], 0.0), -1)
    shares = jax.nn.sigmoid(picked - picked[:, ::-1])
    my_placed = lax.dynamic_index_in_dim(placed, ctx, 0, keepdims=False)
    combine = jnp.sum(jnp.where(my_placed, shares[:, :, None], 0.0), 1)
    combine = combine.reshape(1, rows, 1, experts, 1, CAP)
    eye = jnp.eye(QUARTERS, dtype=f32).reshape(QUARTERS, 1, 1, 1, QUARTERS, 1)
    combine = jnp.broadcast_to(combine * eye, (QUARTERS, rows, nx, experts, QUARTERS, CAP))
    combine = combine.reshape(QUARTERS * rows, peers * QUARTERS * CAP)
    return pl.pallas_call(
        home_kernel,
        out_shape=jax.ShapeDtypeStruct((rows, features), bf16),
        in_specs=[VMEM] * 3,
        out_specs=VMEM,
        compiler_params=limit(total),
        name="combine",
    )(returned, combine, home)


def solution(mesh):
    in_specs = (
        P("ctx", "exp"),
        P("ctx", "exp"),
        P("ctx", "exp"),
        P(None, "exp"),
        P("exp"),
        P("exp", None),
        P("ctx", "exp"),
        P("exp"),
        P("exp", "ctx"),
        P(),
        P(),
        P("exp", "ctx", None),
        P("exp", "ctx", None),
        P("exp", "ctx", None),
        P(("ctx", "exp"), None),
    )
    out_specs = P(("ctx", "exp"), None)
    return jax.shard_map(local, mesh=mesh, in_specs=in_specs, out_specs=out_specs, check_vma=False)
```

```python
import functools

import jax
import jax.numpy as jnp
import numpy as np
from jax import lax
from jax.experimental import pallas as pl
from jax.experimental.pallas import tpu as pltpu
from jax.sharding import PartitionSpec as P

STATE = 16
CONV = 4
EPS = 1e-05
TOP = 2
CAP = 2
CHUNK = 64
QUARTERS = 8

precise = lax.Precision.HIGHEST
f32 = jnp.float32
bf16 = jnp.bfloat16


VMEM = pl.BlockSpec(memory_space=pltpu.VMEM)
SMEM = pl.BlockSpec(memory_space=pltpu.SMEM)
ANY = pl.BlockSpec(memory_space=pltpu.HBM)
MIB = 1024 * 1024


def limit(total):
    return pltpu.CompilerParams(vmem_limit_bytes=min(48, 8 * max(1, total // 256)) * MIB)


def dot(a, b, dims=((1,), (0,)), precision=None):
    return lax.dot_general(a, b, (dims, ((), ())), precision=precision, preferred_element_type=f32)


def partner(shard, axis, mask):
    devices = lax.axis_size(axis)
    return lax.ppermute(shard, axis, [(i, i ^ mask) for i in range(devices)])


def is_first(where, rank):
    return lax.slice(where, (0,), (1,)).reshape((1,) * rank) == 0


def gather_ctx(shard, where):
    if lax.axis_size("ctx") != 2:
        return lax.all_gather(shard, "ctx", axis=0)
    other = partner(shard, "ctx", 1)
    first = is_first(where, shard.ndim)
    return jnp.stack([jnp.where(first, shard, other), jnp.where(first, other, shard)], 0)


def swap_rows(pieces, where):
    if lax.axis_size("ctx") != 2:
        return lax.all_to_all(pieces, "ctx", split_axis=0, concat_axis=0, tiled=True)
    first = is_first(where, pieces.ndim - 1)
    own = jnp.where(first, pieces[0], pieces[1])
    other = partner(jnp.where(first, pieces[1], pieces[0]), "ctx", 1)
    return jnp.stack([jnp.where(first, own, other), jnp.where(first, other, own)], 0)


def token_planes(tokens):
    return [tokens] + [partner(tokens, "exp", mask) for mask in (4, 8, 12)]


def token_pieces(planes, where):
    size = lax.axis_size("exp")
    ctx, exp = [lax.slice(where, (i,), (i + 1,)).reshape(1, 1) for i in (0, 1)]
    near = ((exp >> 3) & 1) == ctx
    keep = jnp.stack([jnp.where(near, planes[i], planes[i + 2]) for i in (0, 1)], 0)
    give = jnp.stack([jnp.where(near, planes[i + 2], planes[i]) for i in (0, 1)], 0)
    both = [(i, i ^ (size | 2)) for i in range(2 * size)]
    found = {
        (0, 0): keep,
        (1, 0): partner(give, "ctx", 1),
        (0, 1): partner(keep, "exp", 2),
        (1, 1): lax.ppermute(give, ("ctx", "exp"), both),
    }
    pieces = []
    for (dx, dy), piece in found.items():
        pieces.append(((dx, dy, 0), piece))
        pieces.append(((dx, dy, 1), partner(piece, "exp", 1)))
    return pieces


def input_kernel(places, rows, where_ref, *refs):
    pieces, (weight_any, keep_ref, send_ref), rest = refs[:8], refs[8:11], refs[11:]
    *own_refs, whole, weight_ref, arrived = rest
    copy = pltpu.make_async_copy(weight_any, weight_ref, arrived)
    copy.start()
    ctx, exp = where_ref[0], where_ref[1]
    for (dx, dy, dk), piece in zip(places, pieces):
        for j in range(2):
            block = (((exp >> 2) & 1) ^ j) * 4 + (((exp >> 1) & 1) ^ dy) * 2 + ((exp & 1) ^ dk)
            whole[block, ctx ^ dx] = piece[j]
    blocks, _, stretch, part = whole.shape
    everything = jnp.concatenate(
        [whole[b].reshape(2 * stretch, part) for b in range(blocks)], axis=1
    )
    copy.wait()
    result = dot(everything, weight_ref[...])
    keep_ref[...] = result
    send_ref[...] = result.astype(bf16)
    for own_ref in own_refs:
        own_rows = 2 * rows
        row = lax.broadcasted_iota(jnp.int32, (own_rows, 2 * stretch), 0)
        column = lax.broadcasted_iota(jnp.int32, (own_rows, 2 * stretch), 1)
        wanted = jnp.where(row >= rows, row - rows + stretch, row) + exp * rows
        pick = (column == wanted).astype(f32).astype(bf16)
        own_ref[...] = dot(pick, everything).astype(bf16)


def input_call(where, pieces, weight, rows, with_own, name):
    stretch, part = pieces[0][1].shape[1:]
    shape = (2 * stretch, weight.shape[1])
    out_shape = [jax.ShapeDtypeStruct(shape, f32), jax.ShapeDtypeStruct(shape, bf16)]
    if with_own:
        out_shape.append(jax.ShapeDtypeStruct((2 * rows, weight.shape[0]), bf16))
    places = tuple(place for place, _ in pieces)
    return pl.pallas_call(
        functools.partial(input_kernel, places, rows),
        out_shape=out_shape,
        in_specs=[SMEM] + [VMEM] * 8 + [ANY],
        out_specs=[VMEM] * len(out_shape),
        scratch_shapes=[
            pltpu.VMEM((8, 2, stretch, part), bf16),
            pltpu.VMEM(weight.shape, bf16),
            pltpu.SemaphoreType.DMA,
        ],
        compiler_params=pltpu.CompilerParams(vmem_limit_bytes=12 * MIB),
        name=name,
    )(where, *[piece for _, piece in pieces], weight)


def conv_kernel(
    own_ref, got_ref, taps_ref, bias_ref, project_ref, mixer_ref, part_ref, padded, mixer_held, left
):
    total, width = own_ref.shape
    inner = (own_ref[...] + got_ref[...].astype(f32)).astype(bf16).astype(f32)
    padded[0:8, :] = jnp.zeros((8, width), f32)
    padded[8 : 8 + total, :] = inner
    filtered = jnp.broadcast_to(bias_ref[...], (total, width))
    for offset in range(CONV):
        first = 8 - (CONV - 1) + offset
        filtered = filtered + taps_ref[offset : offset + 1, :] * padded[first : first + total, :]
    mixer = (filtered * jax.nn.sigmoid(filtered)).astype(bf16)
    mixer_held[...] = mixer
    leaving = pltpu.make_async_copy(mixer_held, mixer_ref, left)
    leaving.start()
    part_ref[...] = dot(project_ref[...], mixer, ((1,), (1,)))
    leaving.wait()


def mixer_kernel(
    homes, group, where_ref, proj_ref, skip_ref, mixer_any, gate_any, got_any, weight_any, *refs
):
    (
        *step_anys, keep_any, send_ref, columns, mixed, mixer_ref, gate_ref, got_ref, weight_ref,
        step_ref, keep_ref, arrived,
    ) = refs
    pairs = [(mixer_any, mixer_ref), (gate_any, gate_ref), (got_any, got_ref)]
    if len(step_anys) == 1:
        pairs.append((step_anys[0], step_ref))
    else:
        stretch = step_anys[0].shape[0]
        for i, step_any in enumerate(step_anys):
            first = pl.multiple_of((where_ref[0] ^ i) * stretch, stretch)
            pairs.append((step_any, step_ref.at[pl.ds(first, stretch)]))
    pairs.append((weight_any, weight_ref))
    copies = [
        pltpu.make_async_copy(source, ref, arrived.at[i]) for i, (source, ref) in enumerate(pairs)
    ]
    for copy in copies:
        copy.start()
    total, width = mixer_ref.shape
    chunk = min(CHUNK, total)
    contexts = total // (homes * group)
    rows = lax.broadcasted_iota(jnp.int32, (chunk, chunk), 0)
    cols = lax.broadcasted_iota(jnp.int32, (chunk, chunk), 1)
    causal = rows >= cols
    ones = causal.astype(f32)
    columns[...] = jnp.sum(proj_ref[...], 0).T
    low = where_ref[1] & 1
    for copy in copies[:-1]:
        copy.wait()

    def step(turn, state):
        start = turn * chunk
        at = pl.ds(start if isinstance(start, int) else pl.multiple_of(start, chunk), chunk)
        decay = dot(ones, step_ref[at, :], precision=precise)
        half = 0.5 * decay[chunk - 1 : chunk, :]
        mixer = mixer_ref[at, :].astype(f32)
        raised = mixer * jnp.exp(decay - half)
        gain = columns[at, :STATE]
        read = columns[at, STATE:]
        scores = jnp.where(causal, dot(read, gain, ((1,), (1,)), precise), 0.0)
        fall = jnp.exp(-half)
        state = state * fall
        reading = jnp.exp(half - decay) * (
            dot(scores, raised, precision=precise) + dot(read, state, precision=precise)
        )
        state = fall * (state + dot(gain, raised, ((0,), (0,)), precise))
        gate = (gate_ref[at, :] + got_ref[at, :].astype(f32)).astype(bf16).astype(f32)
        result = (reading + skip_ref[...] * mixer) * (gate * jax.nn.sigmoid(gate))
        for i in range(chunk // group):
            number = turn * (chunk // group) + i
            home, context = number % homes, number // homes
            place = ((home % 2) * (homes // 2) + home // 2) * contexts + context
            place = place * group
            if not isinstance(place, int):
                place = pl.multiple_of(place, group)
            mixed[pl.ds(place, group), :] = result[i * group : (i + 1) * group, :]
        return state

    state = jnp.zeros((STATE, width), f32)
    turns = total // chunk
    if turns <= 4:
        for turn in range(turns):
            state = step(turn, state)
    else:
        lax.fori_loop(0, turns, step, state)
    part = total // 2
    mine = mixed[pl.ds(pl.multiple_of(low * part, part), part), :].astype(bf16)
    other = mixed[pl.ds(pl.multiple_of((1 - low) * part, part), part), :].astype(bf16)
    copies[-1].wait()
    keep_ref[...] = dot(mine, weight_ref[...]).astype(bf16)
    leaving = pltpu.make_async_copy(keep_ref, keep_any, arrived.at[6])
    leaving.start()
    send_ref[...] = dot(other, weight_ref[...]).astype(bf16)
    leaving.wait()


def pair_kernel(keep_any, got_ref, out_ref, keep_ref, arrived):
    copy = pltpu.make_async_copy(keep_any, keep_ref, arrived)
    copy.start()
    copy.wait()
    out_ref[...] = (keep_ref[...].astype(f32) + got_ref[...].astype(f32)).astype(bf16)


def dispatch_kernel(parts, pieces_ref, tokens_ref, select_ref, residual_ref, out_ref):
    projected = jnp.sum(pieces_ref[...].astype(f32), 0)
    residual = (tokens_ref[...].astype(f32) + projected).astype(bf16)
    residual_ref[...] = residual
    width = residual.shape[1] // parts
    stacked = jnp.concatenate([residual[:, q * width : (q + 1) * width] for q in range(parts)], 0)
    sent = dot(select_ref[...], stacked).astype(bf16)
    for c in range(out_ref.shape[0]):
        out_ref[c] = sent


def expert_kernel(
    contexts, parts, packed, got_ref, scale_ref, gate_any, up_any, down_any, out_ref,
    inputs, sums, held, arrived,
):
    slots, features = inputs.shape
    depth, _, block, _ = held.shape
    count = gate_any.shape[1] // block

    def copies(step):
        slot = step % depth
        return [
            pltpu.make_async_copy(
                ref.at[0, pl.ds(step * block, block)], held.at[slot, i], arrived.at[slot, i]
            )
            for i, ref in enumerate((gate_any, up_any, down_any))
        ]

    for step in range(min(depth - 1, count)):
        for copy in copies(step):
            copy.start()
    lanes = got_ref.shape[2]
    height = got_ref.shape[1]
    homes = slots // (contexts * CAP)
    row = lax.broadcasted_iota(jnp.int32, (slots, height), 0)
    column = lax.broadcasted_iota(jnp.int32, (slots, height), 1)
    cap, home = row % CAP, (row // CAP) % homes
    context = row // (CAP * homes)
    base = (home * parts * contexts + context) * CAP + cap
    for q in range(parts):
        pick = (column == base + q * contexts * CAP).astype(f32).astype(bf16)
        for c in range(contexts):
            first = (c * parts + q) * lanes
            inputs[:, first : first + lanes] = dot(pick, got_ref[c]).astype(bf16)
    wide = inputs[...].astype(f32)
    scale = lax.rsqrt(jnp.mean(wide * wide, -1, keepdims=True) + EPS)
    inputs[...] = (wide * scale * scale_ref[...]).astype(bf16)
    sums[...] = jnp.zeros_like(sums)

    for step in range(count):
        if step + depth - 1 < count:
            for copy in copies(step + depth - 1):
                copy.start()
        slot = step % depth
        gate_copy, up_copy, down_copy = copies(step)
        tokens = inputs[...]
        gate_copy.wait()
        gate = dot(tokens, held[slot, 0], ((1,), (1,)))
        up_copy.wait()
        up = dot(tokens, held[slot, 1], ((1,), (1,)))
        hidden = (gate * jax.nn.sigmoid(gate) * up).astype(bf16)
        down_copy.wait()
        sums[...] += dot(hidden, held[slot, 2])
    if not packed:
        out_ref[...] = sums[...].astype(bf16)
        return
    finished = sums[...].astype(bf16)
    width = features // QUARTERS
    stacked = jnp.concatenate(
        [finished[:, q * width : (q + 1) * width] for q in range(QUARTERS)], 0
    )
    size = slots * QUARTERS
    row = lax.broadcasted_iota(jnp.int32, (size, size), 0)
    column = lax.broadcasted_iota(jnp.int32, (size, size), 1)
    peer, q, cap = row // (QUARTERS * CAP), (row // CAP) % QUARTERS, row % CAP
    pick = (column == q * slots + peer * CAP + cap).astype(f32).astype(bf16)
    out_ref[...] = dot(pick, stacked).astype(bf16)


def home_kernel(returned_ref, combine_ref, home_ref, out_ref):
    rows = home_ref.shape[0]
    mixed = dot(combine_ref[...], returned_ref[...].astype(f32), precision=precise)
    mixed = jnp.concatenate([mixed[q * rows : (q + 1) * rows, :] for q in range(QUARTERS)], 1)
    out_ref[...] = (home_ref[...].astype(f32) + mixed).astype(bf16)


def local(
    tokens,
    input_weight,
    gate_weight,
    conv_weight,
    conv_bias,
    state_weight,
    step_size,
    skip_gain,
    output_weight,
    norm_gain,
    router_weight,
    expert_gate,
    expert_up,
    expert_down,
    expert_ids,
):
    nx, ne = lax.axis_size("ctx"), lax.axis_size("exp")
    ctx, exp = lax.axis_index("ctx"), lax.axis_index("exp")
    stretch, part = tokens.shape
    total = stretch * nx
    rows = expert_ids.shape[0]
    width = input_weight.shape[1]
    columns = output_weight.shape[1]
    experts = router_weight.shape[1]
    where = lax.optimization_barrier(jnp.stack([ctx, exp]).astype(jnp.int32))

    if nx == 2 and ne == 16:
        planes = token_planes(tokens)
        pieces = token_pieces(planes, where)
        x_own, x_send = input_call(where, pieces, input_weight, rows, False, "input_projection")
        x_send, gate_weight = lax.optimization_barrier((x_send, gate_weight))
        z_own, z_send, own_tokens = input_call(
            where, pieces, gate_weight, rows, True, "gate_projection"
        )
        x_got, z_send, step_size, expert_ids, where = lax.optimization_barrier(
            (partner(x_send, "ctx", 1), z_send, step_size, expert_ids, where)
        )
        z_got = partner(z_send, "ctx", 1)
    else:
        stretch_whole = lax.all_gather(tokens, "exp", axis=1, tiled=True)
        everything = lax.all_to_all(
            stretch_whole, "ctx", split_axis=1, concat_axis=0, tiled=True
        )
        own_tokens = lax.dynamic_index_in_dim(
            everything.reshape(nx, ne, rows, columns), exp, 1, keepdims=False
        ).reshape(nx * rows, columns)
        x_own = lax.psum(dot(everything, input_weight), "ctx")
        z_own = lax.psum(dot(everything, gate_weight), "ctx")
        x_got = z_got = jnp.zeros((total, width), bf16)

    everyone = gather_ctx(expert_ids, where)
    chosen = (everyone[..., None] == jnp.arange(experts, dtype=jnp.int32)).astype(jnp.int32)
    hits = chosen.reshape(nx, rows * TOP, experts)
    earlier = jnp.cumsum(hits, 1) - hits
    slot = jnp.sum(earlier * hits, -1).reshape(nx, rows, TOP)
    place = everyone * CAP + slot
    placed = place[..., None] == jnp.arange(experts * CAP, dtype=jnp.int32)
    parts = max(1, 16 // (nx * CAP))
    taken = jnp.any(placed, 2).reshape(nx, rows, experts, CAP)
    same_part = np.eye(parts, dtype=bool)[None, :, None, None, :, None, None]
    same_ctx = np.eye(nx, dtype=bool)[None, None, :, None, None, :, None]
    by_expert = taken.transpose(2, 3, 0, 1)[:, None, None, :, None, :, :]
    select = (by_expert & same_part & same_ctx).astype(bf16)
    slots = experts * nx * CAP
    select = select.reshape(slots * parts, parts * nx * rows)
    if nx == 2:
        steps = (step_size, partner(step_size, "ctx", 1))
    else:
        steps = (lax.all_gather(step_size, "ctx", axis=0, tiled=True),)

    mixer_in, part_sum = pl.pallas_call(
        conv_kernel,
        out_shape=[
            jax.ShapeDtypeStruct((total, width), bf16),
            jax.ShapeDtypeStruct((2 * STATE, total), f32),
        ],
        in_specs=[VMEM] * 5,
        out_specs=[ANY, VMEM],
        scratch_shapes=[
            pltpu.VMEM((8 + total, width), f32),
            pltpu.VMEM((total, width), bf16),
            pltpu.SemaphoreType.DMA,
        ],
        compiler_params=limit(total),
        name="convolution",
    )(x_own, x_got, conv_weight, conv_bias[None, :], state_weight.T)

    groups = [[2 * i + k for i in range(ne // 2)] for k in range(2)]
    part_sum = part_sum + partner(part_sum, "exp", 1)
    projections = lax.all_to_all(
        jnp.broadcast_to(part_sum[None], (ne // 2,) + part_sum.shape),
        "exp", split_axis=0, concat_axis=0, tiled=True, axis_index_groups=groups,
    )
    projections, select = lax.optimization_barrier((projections, select))
    keep, send = pl.pallas_call(
        functools.partial(mixer_kernel, ne, rows),
        out_shape=[jax.ShapeDtypeStruct((total // 2, columns), bf16)] * 2,
        in_specs=[SMEM] + [VMEM] * 2 + [ANY] * (4 + len(steps)),
        out_specs=[ANY, VMEM],
        scratch_shapes=[
            pltpu.VMEM((total, 2 * STATE), f32),
            pltpu.VMEM((total, width), f32),
            pltpu.VMEM((total, width), bf16),
            pltpu.VMEM((total, width), f32),
            pltpu.VMEM((total, width), bf16),
            pltpu.VMEM(output_weight.shape, bf16),
            pltpu.VMEM((total, width), f32),
            pltpu.VMEM((total // 2, columns), bf16),
            pltpu.SemaphoreType.DMA((7,)),
        ],
        compiler_params=limit(2 * total),
        name="state_scan_and_output",
    )(
        where, projections, skip_gain[None, :],
        mixer_in, z_own, z_got, output_weight, *steps,
    )

    pair = pl.pallas_call(
        pair_kernel,
        out_shape=jax.ShapeDtypeStruct(send.shape, bf16),
        in_specs=[ANY, VMEM],
        out_specs=VMEM,
        scratch_shapes=[pltpu.VMEM(send.shape, bf16), pltpu.SemaphoreType.DMA],
        compiler_params=limit(total),
        name="pair_sum",
    )(keep, partner(send, "exp", 1))
    sums = lax.all_to_all(
        pair.reshape(ne // 2, nx * rows, columns),
        "exp", split_axis=0, concat_axis=0, tiled=True, axis_index_groups=groups,
    )

    residual, outgoing = pl.pallas_call(
        functools.partial(dispatch_kernel, parts),
        out_shape=[
            jax.ShapeDtypeStruct((nx * rows, columns), bf16),
            jax.ShapeDtypeStruct((nx, slots * parts, columns // parts), bf16),
        ],
        in_specs=[VMEM] * 3,
        out_specs=[VMEM] * 2,
        compiler_params=limit(total),
        name="residual_and_dispatch",
    )(sums, own_tokens, select)
    arrived = lax.all_to_all(
        outgoing.reshape(nx * experts, nx * CAP * parts, columns // parts),
        ("ctx", "exp"), split_axis=0, concat_axis=0, tiled=True,
    ).reshape(nx, slots * parts, columns // parts)

    hidden, features = expert_gate.shape[1:]
    block = next(b for b in (512, 448, 256, 128, 64, 32, 16) if hidden % b == 0)
    packed = nx == 2
    unit = features // QUARTERS
    peers = nx * experts
    done_shape = (peers * CAP * QUARTERS, unit) if packed else (slots, features)
    depth = 3 if packed else 2
    finished = pl.pallas_call(
        functools.partial(expert_kernel, nx, parts, packed),
        out_shape=jax.ShapeDtypeStruct(done_shape, bf16),
        in_specs=[VMEM] * 2 + [ANY] * 3,
        out_specs=VMEM,
        scratch_shapes=[
            pltpu.VMEM((slots, features), bf16),
            pltpu.VMEM((slots, features), f32),
            pltpu.VMEM((depth, 3, block, features), bf16),
            pltpu.SemaphoreType.DMA((depth, 3)),
        ],
        compiler_params=pltpu.CompilerParams(vmem_limit_bytes=52 * MIB),
        cost_estimate=pl.CostEstimate(
            flops=6 * slots * hidden * features,
            bytes_accessed=6 * hidden * features,
            transcendentals=slots * hidden,
        ),
        name="experts",
    )(arrived, norm_gain[None, :], expert_gate, expert_up, expert_down)
    if not packed:
        finished = finished.reshape(peers, CAP, QUARTERS, unit).transpose(0, 2, 1, 3)
    returned = lax.all_to_all(
        finished.reshape(peers, QUARTERS * CAP, unit),
        ("ctx", "exp"), split_axis=0, concat_axis=0, tiled=True,
    ).reshape(peers * QUARTERS * CAP, unit)

    home = swap_rows(residual.reshape(nx, rows, columns), where)
    home = home.transpose(1, 0, 2).reshape(rows, features)
    wide = home.astype(f32)
    scale = lax.rsqrt(jnp.mean(wide * wide, -1, keepdims=True) + EPS)
    normed = (wide * scale * norm_gain[None, :]).astype(bf16)
    logits = dot(normed, router_weight)
    my_choice = expert_ids[:, :, None] == jnp.arange(experts, dtype=jnp.int32)
    picked = jnp.sum(jnp.where(my_choice, logits[:, None, :], 0.0), -1)
    shares = jax.nn.sigmoid(picked - picked[:, ::-1])
    my_placed = lax.dynamic_index_in_dim(placed, ctx, 0, keepdims=False)
    combine = jnp.sum(jnp.where(my_placed, shares[:, :, None], 0.0), 1)
    combine = combine.reshape(1, rows, 1, experts, 1, CAP)
    eye = np.eye(QUARTERS, dtype=np.float32).reshape(QUARTERS, 1, 1, 1, QUARTERS, 1)
    combine = jnp.broadcast_to(combine * eye, (QUARTERS, rows, nx, experts, QUARTERS, CAP))
    combine = combine.reshape(QUARTERS * rows, peers * QUARTERS * CAP)
    return pl.pallas_call(
        home_kernel,
        out_shape=jax.ShapeDtypeStruct((rows, features), bf16),
        in_specs=[VMEM] * 3,
        out_specs=VMEM,
        compiler_params=limit(total),
        name="combine",
    )(returned, combine, home)


def solution(mesh):
    in_specs = (
        P("ctx", "exp"),
        P("ctx", "exp"),
        P("ctx", "exp"),
        P(None, "exp"),
        P("exp"),
        P("exp", None),
        P("ctx", "exp"),
        P("exp"),
        P("exp", "ctx"),
        P(),
        P(),
        P("exp", "ctx", None),
        P("exp", "ctx", None),
        P("exp", "ctx", None),
        P(("ctx", "exp"), None),
    )
    out_specs = P(("ctx", "exp"), None)
    return jax.shard_map(local, mesh=mesh, in_specs=in_specs, out_specs=out_specs, check_vma=False)
```
